32 devices in a mesh: region: 2 (over y), dom: 4 (over x, core), sub: 4 (over z).
Axes of the slice: x: 2, y: 2, z: 4, core: 2. Of those that a mesh axis runs over, the one named last changes fastest.
Arguments:
- features: bfloat16 [16384, 256], P(('region', 'dom', 'sub')), parts along dimension 0, may hold values from -6 to 6
- local_blocks: int32 [128, 4], P(('region', 'dom', 'sub')), parts along dimension 0, may hold values from 0 to 15
- local_matrix: bfloat16 [128, 4, 128, 128], P(('region', 'dom', 'sub')), parts along dimension 0, may hold values from -0.1875 to 0.1875
- remote_blocks: int32 [128, 4], P(('region', 'dom', 'sub')), parts along dimension 0, may hold values from 0 to 3
- remote_matrix: bfloat16 [128, 4, 128, 128], P(('region', 'dom', 'sub')), parts along dimension 0, may hold values from -0.1875 to 0.1875
- send_blocks: int32 [32, 2, 2], P(('region', 'dom', 'sub')), parts along dimension 0, may hold values from 0 to 3
- send_counts: int32 [32, 2], P(('region', 'dom', 'sub')), parts along dimension 0, may hold values from 1 to 2
- partner: int32 [4, 4], P('region'), parts along dimension 0, may hold values from 0 to 3, as said below
- self_weight: bfloat16 [2, 256, 512], replicated, may hold values from -0.375 to 0.375
- neighbor_weight: bfloat16 [2, 256, 512], replicated, may hold values from -0.375 to 0.375
- output_weight: bfloat16 [2, 512, 256], replicated, may hold values from -0.25 to 0.25
- output_cotangent: bfloat16 [16384, 256], P(('region', 'dom', 'sub')), parts along dimension 0, may hold values from -6 to 6
Outputs:
- updated: bfloat16 [16384, 256], P(('region', 'dom', 'sub')), parts along dimension 0
- feature_grad: float32 [16384, 256], P(('region', 'dom', 'sub')), parts along dimension 0
- self_grad: float32 [4, 256, 512], P('region'), parts along dimension 0
- neighbor_grad: float32 [4, 256, 512], P('region'), parts along dimension 0
- output_grad: float32 [4, 512, 256], P('region'), parts along dimension 0
The draws below stay inside these ranges and needn't reach their ends.
There are 2 independent parts, one for each index of `region`. The reference program is written for one: setup_inputs(seed, part) draws one part's arguments, and reference() takes and returns one part's arrays. A program takes and returns all parts, laid end to end along the dimension named above; an argument that names none is the same for every part. Nothing has to cross between parts.
Inputs may be any that keep to these rules, and one draw needn't show every extreme that they name: Every round is a perfect matching of the 4 partitions (partner[r, partner[r, d]] = d, never d itself), and no two partitions are matched in two rounds.
All inputs are finite; a program needn't handle non-finite values.
Results may differ from the reference program's by a relative error of at most 0.009.
Values may be sent and summed in bfloat16 or wider, within the bound.
A program may use at most 64 MiB of HBM per device.

```python
import jax
import jax.numpy as jnp

D = 256
HID = 512
BLK = 128
LK = 4
BK = 4
SEND = 2
L = 2
BPS = 4
R = 2
DEVS = 16
BPD = 16
NB = 64
NODES = 8192
N_DOM = 4
N_SUB = 4


def draw_partner(key, part):
    key = jax.random.fold_in(key, 5)
    colors = jax.random.permutation(key, N_DOM - 1)[:R] + 1
    domains = jnp.arange(N_DOM, dtype=jnp.int32)
    return jnp.bitwise_xor(domains[None, :], colors[:, None].astype(jnp.int32)).astype(jnp.int32)


def place_ends(values, own_key, least, largest):
    shape = values.shape
    place = [jax.random.randint(jax.random.fold_in(own_key, axis), (), 0, shape[axis]) for axis in range(len(shape))]
    values = values.at[tuple(place)].set(least)
    longest = shape.index(max(shape))
    place[longest] = (place[longest] + 1) % shape[longest]
    return values.at[tuple(place)].set(largest)


def block_levels(stream_key, dims, pieces, smallest, top_value):
    def one(axis_at, shards_of):
        steps = jax.random.uniform(jax.random.fold_in(jax.random.fold_in(stream_key, 6), axis_at), (shards_of,), jnp.float32, smallest / len(pieces), top_value / len(pieces))
        return jnp.repeat(jnp.exp(steps), dims[axis_at] // shards_of).reshape((-1,) + (1,) * (len(dims) - axis_at - 1))

    gain = one(*pieces[0])
    for cut in pieces[1:]:
        gain = gain * one(*cut)
    return gain


def gaussian(own_key, shape, scale, limit, cuts=(), kind=jnp.bfloat16):
    drawn = scale * jax.random.normal(own_key, shape, jnp.float32)
    if cuts:
        drawn = drawn * block_levels(own_key, shape, cuts, -0.22, 0.18)
    return jnp.clip(drawn, -limit, limit).astype(kind)


def setup_inputs(seed: int = 0, part: int = 0) -> dict:
    keys = jax.random.split(jax.random.key(seed), 13)
    part_keys = jax.random.split(jax.random.fold_in(keys[12], part), 13)
    features = gaussian(part_keys[0], (NODES, D), 1.0, 6.0, ((0, 16),))
    local_blocks = place_ends(jax.random.randint(part_keys[1], (NB, LK), 0, BPD), jax.random.fold_in(part_keys[1], 1), 0, BPD - 1).astype(jnp.int32)
    local_matrix = gaussian(part_keys[2], (NB, LK, BLK, BLK), (BLK * (LK + BK)) ** -0.5, 0.1875, ((0, 16),))
    remote_blocks = place_ends(jax.random.randint(part_keys[3], (NB, BK), 0, R * SEND), jax.random.fold_in(part_keys[3], 1), 0, (R * SEND) - 1).astype(jnp.int32)
    remote_matrix = gaussian(part_keys[4], (NB, BK, BLK, BLK), (BLK * (LK + BK)) ** -0.5, 0.1875, ((0, 16),))
    send_blocks = place_ends(jax.random.randint(part_keys[5], (DEVS, R, SEND), 0, BPS), jax.random.fold_in(part_keys[5], 1), 0, BPS - 1).astype(jnp.int32)
    send_counts = place_ends(jax.random.randint(part_keys[6], (DEVS, R), 1, SEND + 1), jax.random.fold_in(part_keys[6], 1), 1, SEND).astype(jnp.int32)
    partner = draw_partner(jax.random.fold_in(jax.random.fold_in(keys[12], part), 71), part)
    self_weight = gaussian(keys[8], (L, D, HID), D ** -0.5, 0.375)
    neighbor_weight = gaussian(keys[9], (L, D, HID), D ** -0.5, 0.375)
    output_weight = gaussian(keys[10], (L, HID, D), HID ** -0.5, 0.25)
    output_cotangent = gaussian(part_keys[11], (NODES, D), 1.0, 6.0, ((0, 16),))
    return {"features": features, "local_blocks": local_blocks, "local_matrix": local_matrix, "remote_blocks": remote_blocks, "remote_matrix": remote_matrix, "send_blocks": send_blocks, "send_counts": send_counts, "partner": partner, "self_weight": self_weight, "neighbor_weight": neighbor_weight, "output_weight": output_weight, "output_cotangent": output_cotangent}


def remote_layout(send_blocks, send_counts, partner):
    devices = jnp.arange(DEVS, dtype=jnp.int32)
    home_dom = devices // N_SUB
    home_sub = devices % N_SUB
    round_ids = jnp.arange(R, dtype=jnp.int32)
    sender = (partner[:, home_dom].T * N_SUB + home_sub[:, None]).astype(jnp.int32)
    sent_local = send_blocks[sender, round_ids[None, :]]
    source_block = sender[:, :, None] * BPS + sent_local
    alive = jnp.arange(SEND, dtype=jnp.int32)[None, None, :] < send_counts[sender, round_ids[None, :]][:, :, None]
    return source_block.reshape(DEVS, R * SEND).astype(jnp.int32), alive.reshape(DEVS, R * SEND)


def reference(features, local_blocks, local_matrix, remote_blocks, remote_matrix, send_blocks, send_counts, partner, self_weight, neighbor_weight, output_weight, output_cotangent):
    owner = (jnp.arange(NB, dtype=jnp.int32) // BPS).astype(jnp.int32)
    local_glob = ((jnp.arange(NB, dtype=jnp.int32) // BPD) * BPD)[:, None] + local_blocks
    source_block, alive = remote_layout(send_blocks, send_counts, partner)
    remote_glob = source_block[owner[:, None], remote_blocks]
    remote_alive = alive[owner[:, None], remote_blocks]
    scale = 1.0 / (NODES ** 0.5)
    saved = []
    state = features
    for layer_id in range(L):
        blocks = state.reshape(NB, BLK, D)
        near = blocks[local_glob].astype(jnp.float32)
        far = blocks[remote_glob].astype(jnp.float32) * remote_alive[:, :, None, None].astype(jnp.float32)
        total = jnp.einsum('nkab,nkbd->nad', local_matrix.astype(jnp.float32), near)
        total = total + jnp.einsum('nkab,nkbd->nad', remote_matrix.astype(jnp.float32), far)
        aggregate = total.reshape(NODES, D).astype(jnp.bfloat16)
        preact = jnp.dot(state, self_weight[layer_id], preferred_element_type=jnp.float32) + jnp.dot(aggregate, neighbor_weight[layer_id], preferred_element_type=jnp.float32)
        hidden = jax.nn.silu(preact).astype(jnp.bfloat16)
        result = (state.astype(jnp.float32) + jnp.dot(hidden, output_weight[layer_id], preferred_element_type=jnp.float32)).astype(jnp.bfloat16)
        saved.append((state, aggregate, preact, hidden))
        state = result
    updated = state
    upstream = output_cotangent.astype(jnp.float32)
    grads_self = [None] * L
    grads_neighbor = [None] * L
    grads_output = [None] * L
    for layer_id in range(L - 1, -1, -1):
        state, aggregate, preact, hidden = saved[layer_id]
        cot = upstream.astype(jnp.bfloat16)
        grads_output[layer_id] = jnp.dot(hidden.T, cot, preferred_element_type=jnp.float32) * scale
        grad_hidden = jnp.dot(cot, output_weight[layer_id].T, preferred_element_type=jnp.float32)
        logistic = jax.nn.sigmoid(preact)
        grad_preact = (grad_hidden * logistic * (1.0 + preact * (1.0 - logistic))).astype(jnp.bfloat16)
        grads_self[layer_id] = jnp.dot(state.T, grad_preact, preferred_element_type=jnp.float32) * scale
        grads_neighbor[layer_id] = jnp.dot(aggregate.T, grad_preact, preferred_element_type=jnp.float32) * scale
        grad_aggregate = jnp.dot(grad_preact, neighbor_weight[layer_id].T, preferred_element_type=jnp.float32).astype(jnp.bfloat16)
        grad_blocks = grad_aggregate.reshape(NB, BLK, D).astype(jnp.float32)
        near_terms = jnp.einsum('nkab,nad->nkbd', local_matrix.astype(jnp.float32), grad_blocks)
        near_sum = jax.ops.segment_sum(near_terms.reshape(NB * LK, BLK, D), local_glob.reshape(-1), num_segments=NB)
        far_terms = jnp.einsum('nkab,nad->nkbd', remote_matrix.astype(jnp.float32), grad_blocks)
        slot_ids = (owner[:, None] * (R * SEND) + remote_blocks).reshape(-1).astype(jnp.int32)
        slot_grad = jax.ops.segment_sum(far_terms.reshape(NB * BK, BLK, D), slot_ids, num_segments=DEVS * R * SEND).astype(jnp.bfloat16)
        slot_vals = slot_grad.astype(jnp.float32) * alive.reshape(-1)[:, None, None].astype(jnp.float32)
        far_sum = jax.ops.segment_sum(slot_vals, source_block.reshape(-1), num_segments=NB)
        upstream = upstream + jnp.dot(grad_preact, self_weight[layer_id].T, preferred_element_type=jnp.float32) + near_sum.reshape(NODES, D) + far_sum.reshape(NODES, D)
    return updated, upstream, jnp.stack(grads_self), jnp.stack(grads_neighbor), jnp.stack(grads_output)
```

```python
import functools

import jax
import jax.numpy as jnp
from jax import lax
from jax.experimental import pallas as pl
from jax.experimental.pallas import tpu as pltpu
from jax.sharding import PartitionSpec as P

F32 = jnp.float32
BF16 = jnp.bfloat16
ROWS = 16


def dot(a, b):
    return jnp.dot(a, b, preferred_element_type=F32)


def dot_nt(a, b):
    return lax.dot_general(a, b, (((1,), (1,)), ((), ())), preferred_element_type=F32)


def dot_tn(a, b):
    return lax.dot_general(a, b, (((0,), (0,)), ((), ())), preferred_element_type=F32)


def kernel(
    n_dom, n_sub, scale,
    lb, rb, sb, sc, pt,
    x_ref, lm, rm, ws, wn, wo, ct,
    upd, fg, gs, gn, go,
    adj, far, st, ag, agg, pre, hid, own,
    bsend, brecv, rsend, rrecv, rs,
    wsend, wrecv, wfull, zpart, zrecv, zfull,
    ag_s, ag_r, bf_s, bf_r, bb_s, bb_r, rs_s, rs_r,
    wd_s, wd_r, wz_s, wz_r, we_s, we_r, wf_s, wf_r,
):
    layers = ws.shape[0]
    nb, blk = lm.shape[0], lm.shape[2]
    width = x_ref.shape[1]
    rounds, slots = sb.shape[1], sb.shape[2]
    here = nb * blk
    chunks = ag_r.shape[2]
    crow = here // chunks
    dom = lax.axis_index("dom")
    sub = lax.axis_index("sub")
    pending = []

    def remote(src, dst, send, recv, axis, peer):
        return pltpu.make_async_remote_copy(
            src_ref=src, dst_ref=dst, send_sem=send, recv_sem=recv,
            device_id={axis: peer}, device_id_type=pl.DeviceIdType.MESH,
        )

    def start(copy, cond=None):
        if cond is None:
            copy.start()
        else:
            pl.when(cond)(copy.start)
        pending.append((copy, cond))

    barrier = pltpu.get_barrier_semaphore()
    for axis, me, n in (("dom", dom, n_dom), ("sub", sub, n_sub)):
        for d in range(1, n):
            pl.semaphore_signal(
                barrier, inc=1, device_id={axis: lax.rem(me + d, n)},
                device_id_type=pl.DeviceIdType.MESH,
            )
    pl.semaphore_wait(barrier, n_dom + n_sub - 2)

    right, left = jnp.minimum(sub + 1, n_sub - 1), jnp.maximum(sub - 1, 0)
    has_right, has_left = sub < n_sub - 1, sub > 0

    def gather_start(l):
        for c in range(chunks):
            part = st.at[l, pl.ds(c * crow, crow)]
            there = ag.at[l, sub, pl.ds(c * crow, crow)]
            start(remote(part, there, ag_s.at[l, sub, c, 0], ag_r.at[l, sub, c], "sub", right), has_right)
            start(remote(part, there, ag_s.at[l, sub, c, 1], ag_r.at[l, sub, c], "sub", left), has_left)

    def gather_step(l, d):
        for c in range(chunks):
            for src, ok, to, more, way in (
                (sub - d, sub - d >= 0, right, has_right, 0),
                (sub + d, sub + d < n_sub, left, has_left, 1),
            ):
                at = jnp.clip(src, 0, n_sub - 1)
                part = ag.at[l, at, pl.ds(c * crow, crow)]
                copy = remote(part, part, ag_s.at[l, at, c, way], ag_r.at[l, at, c], "sub", to)
                pl.when(ok)(copy.wait_recv)
                start(copy, jnp.logical_and(ok, more))

    def picks(p, j):
        out = []
        for b in range(nb):
            one = jnp.float32(0.0)
            for r in range(rounds):
                good = (pt[r, dom] == p) & (j < sc[0, r]) & (sb[0, r, j] == b)
                one = one + jnp.where(good, 1.0, 0.0)
            out.append(one)
        return out

    def boundary_start(l):
        for d in range(1, n_dom):
            p = lax.rem(dom + d, n_dom)
            for j in range(slots):
                ones = picks(p, j)
                total = jnp.zeros((blk, width), F32)
                for b in range(nb):
                    total = total + st[l, b * blk:(b + 1) * blk, :].astype(F32) * ones[b]
                bsend[l, p, j * blk:(j + 1) * blk, :] = total.astype(BF16)
            start(remote(bsend.at[l, p], brecv.at[l, dom], bf_s.at[l, p], bf_r.at[l, dom], "dom", p))

    def arrive(buf, sems, l, axis, me, n):
        for d in range(1, n):
            src = lax.rem(me + n - d, n)
            remote(buf.at[l, src], buf.at[l, src], sems.at[l, src], sems.at[l, src], axis, src).wait_recv()

    def build(matrix, column, out, count):
        @pl.loop(0, count)
        def _(t):
            at = pl.multiple_of(t * blk, blk)
            for b in range(nb):
                total = jnp.zeros((blk, blk), F32)
                for k in range(matrix.shape[1]):
                    hit = jnp.where(column(b, k) == t, 1.0, 0.0)
                    total = total + matrix[b, k].astype(F32) * hit
                out[b * blk:(b + 1) * blk, pl.ds(at, blk)] = total.astype(BF16)

    def far_column(b, k):
        slot = rb[b, k]
        r = lax.div(slot, slots)
        return pt[r, dom] * slots + (slot - r * slots)

    st[0] = x_ref[...]
    for l in range(layers):
        gather_start(l)
        boundary_start(l)
        ag[l, sub] = st[l]
        brecv[l, dom] = jnp.zeros(brecv.shape[2:], BF16)
        if l == 0:
            build(lm, lambda b, k: lb[b, k], adj, n_sub * nb)
            build(rm, far_column, far, n_dom * slots)
        gather_step(l, 1)
        pre[l] = dot(st[l], ws[l])
        arrive(brecv, bf_r, l, "dom", dom, n_dom)
        total = dot(far[...], brecv[l].reshape(-1, width))
        for d in range(2, n_sub):
            gather_step(l, d)
        total = total + dot(adj[...], ag[l].reshape(-1, width))
        agg[l] = total.astype(BF16)
        preact = pre[l] + dot(agg[l], wn[l])
        pre[l] = preact
        hid[l] = (preact / (1.0 + jnp.exp(-preact))).astype(BF16)
        result = (st[l].astype(F32) + dot(hid[l], wo[l])).astype(BF16)
        if l + 1 < layers:
            st[l + 1] = result
        else:
            upd[...] = result

    wrows = wsend.shape[2]
    zrows = zpart.shape[2]

    def weights_start(l, cot, gp):
        tall = jnp.concatenate(
            [dot_tn(st[l], gp), dot_tn(agg[l], gp), dot_tn(cot, hid[l])], axis=0
        ).astype(BF16)
        for p in range(n_dom):
            wsend[l, p] = tall[p * wrows:(p + 1) * wrows]
        for d in range(1, n_dom):
            p = lax.rem(dom + d, n_dom)
            start(remote(wsend.at[l, p], wrecv.at[l, dom], wd_s.at[l, p], wd_r.at[l, dom], "dom", p))

    def weights_dom(l):
        arrive(wrecv, wd_r, l, "dom", dom, n_dom)
        total = wsend[l, dom].astype(F32)
        for d in range(1, n_dom):
            total = total + wrecv[l, lax.rem(dom + d, n_dom)].astype(F32)
        total = total.astype(BF16)
        for s in range(n_sub):
            low, high = min(s * zrows, wrows), min((s + 1) * zrows, wrows)
            if high > low:
                zpart[l, s, :high - low] = total[low:high]
            if high - low < zrows:
                zpart[l, s, high - low:] = jnp.zeros((zrows - high + low, total.shape[1]), BF16)
        for d in range(1, n_sub):
            s = lax.rem(sub + d, n_sub)
            start(remote(zpart.at[l, s], zrecv.at[l, sub], wz_s.at[l, s], wz_r.at[l, sub], "sub", s))

    def weights_sub(l):
        arrive(zrecv, wz_r, l, "sub", sub, n_sub)
        total = zpart[l, sub].astype(F32)
        for d in range(1, n_sub):
            total = total + zrecv[l, lax.rem(sub + d, n_sub)].astype(F32)
        zfull[l, sub] = total.astype(BF16)
        for d in range(1, n_sub):
            s = lax.rem(sub + d, n_sub)
            start(remote(zfull.at[l, sub], zfull.at[l, sub], we_s.at[l, s], we_r.at[l, sub], "sub", s))

    def weights_back(l):
        arrive(zfull, we_r, l, "sub", sub, n_sub)
        wfull[l, dom] = zfull[l].reshape(n_sub * zrows, -1)[:wrows]
        for d in range(1, n_dom):
            p = lax.rem(dom + d, n_dom)
            start(remote(wfull.at[l, dom], wfull.at[l, dom], wf_s.at[l, p], wf_r.at[l, dom], "dom", p))

    def weights_done(l):
        arrive(wfull, wf_r, l, "dom", dom, n_dom)
        tall = wfull[l].reshape(n_dom * wrows, -1).astype(F32) * scale
        gs[l] = tall[:width]
        gn[l] = tall[width:2 * width]
        go[l] = tall[2 * width:].T

    def reduce_start(l, ga):
        for d in range(n_sub - 1, -1, -1):
            for way in (0, 1) if d else (0,):
                raw = sub - d if way else sub + d
                ok = raw >= 0 if way else raw < n_sub
                t = jnp.clip(raw, 0, n_sub - 1)

                @pl.when(ok)
                def _(t=t):
                    own[t] = dot_tn(adj[:, pl.ds(pl.multiple_of(t * here, here), here)], ga)

                if d:
                    edge = sub == (n_sub - 1 if way else 0)
                    reduce_send(l, t, way, jnp.logical_and(ok, edge), False)

    def reduce_send(l, t, way, cond, add):
        to = left if way else right
        for c in range(chunks):
            rows = pl.ds(c * crow, crow)
            part = rs.at[l, t, rows]
            land = jnp.where(t == to, n_sub, t) if way else t
            copy = remote(part, rs.at[l, land, rows], rs_s.at[l, t, c], rs_r.at[l, land, c], "sub", to)

            @pl.when(cond)
            def _(t=t, rows=rows, part=part, c=c):
                value = own[t, rows]
                if add:
                    remote(part, part, rs_s.at[l, t, c], rs_r.at[l, t, c], "sub", to).wait_recv()
                    value = value + rs[l, t, rows].astype(F32)
                rs[l, t, rows] = value.astype(BF16)

            start(copy, cond)

    def reduce_finish(l):
        for d in range(n_sub - 1, 0, -1):
            for way in (0, 1):
                raw = sub - d if way else sub + d
                ok = raw >= 0 if way else raw < n_sub
                inner = has_right if way else has_left
                reduce_send(l, jnp.clip(raw, 0, n_sub - 1), way, jnp.logical_and(ok, inner), True)

    def reduce_last(l):
        for cond, slot in ((has_left, sub), (has_right, n_sub)):
            @pl.when(cond)
            def _(slot=slot):
                for c in range(chunks):
                    rows = pl.ds(c * crow, crow)
                    part = rs.at[l, slot, rows]
                    remote(part, part, rs_r.at[l, slot, c], rs_r.at[l, slot, c], "sub", left).wait_recv()
                    own[sub, rows] += rs[l, slot, rows].astype(F32)
        return own[sub]

    fg[...] = ct[...].astype(F32)
    for l in range(layers - 1, -1, -1):
        cot = fg[...].astype(BF16)
        preact = pre[l]
        logistic = 1.0 / (1.0 + jnp.exp(-preact))
        gp = (dot_nt(cot, wo[l]) * logistic * (1.0 + preact * (1.0 - logistic))).astype(BF16)
        ga = dot_nt(gp, wn[l]).astype(BF16)
        reduce_start(l, ga)
        rsend[l] = dot_tn(far[...], ga).astype(BF16).reshape(rsend.shape[1:])
        for d in range(1, n_dom):
            p = lax.rem(dom + d, n_dom)
            start(remote(rsend.at[l, p], rrecv.at[l, dom], bb_s.at[l, p], bb_r.at[l, dom], "dom", p))
        weights_start(l, cot, gp)
        if l + 1 < layers:
            weights_dom(l + 1)
        upstream = fg[...] + dot_nt(gp, ws[l])
        reduce_finish(l)
        if l + 1 < layers:
            weights_sub(l + 1)
        fg[...] = upstream
        arrive(rrecv, bb_r, l, "dom", dom, n_dom)
        for d in range(1, n_dom):
            p = lax.rem(dom + d, n_dom)
            for j in range(slots):
                ones = picks(p, j)
                slot = rrecv[l, p, j * blk:(j + 1) * blk, :].astype(F32)
                for b in range(nb):
                    fg[b * blk:(b + 1) * blk, :] += slot * ones[b]
        if l == 0:
            weights_dom(l)
        near = reduce_last(l)
        fg[...] = fg[...] + near
        if l + 1 < layers:
            weights_back(l + 1)
    weights_sub(0)
    for l in range(layers - 1, 0, -1):
        weights_done(l)
    weights_back(0)
    weights_done(0)
    for copy, cond in pending:
        if cond is None:
            copy.wait_send()
        else:
            pl.when(cond)(copy.wait_send)


def local(features, local_blocks, local_matrix, remote_blocks, remote_matrix, send_blocks,
          send_counts, partner, self_weight, neighbor_weight, output_weight, output_cotangent):
    n_dom, n_sub = lax.axis_size("dom"), lax.axis_size("sub")
    layers, width, units = self_weight.shape
    here = features.shape[0]
    nb, blk = local_matrix.shape[0], local_matrix.shape[2]
    slots = send_blocks.shape[2]
    scale = 1.0 / (here * n_dom * n_sub) ** 0.5
    chunks = 2
    wrows = 3 * width // n_dom
    zrows = -(-wrows // (n_sub * ROWS)) * ROWS
    vmem, smem = pl.BlockSpec(memory_space=pltpu.VMEM), pl.BlockSpec(memory_space=pltpu.SMEM)
    dma = pltpu.SemaphoreType.DMA
    edge = (layers, n_dom, slots * blk, width)
    tall = (layers, n_dom, wrows, units)
    small = (layers, n_sub, zrows, units)
    return pl.pallas_call(
        functools.partial(kernel, n_dom, n_sub, scale),
        out_shape=(
            jax.ShapeDtypeStruct((here, width), BF16),
            jax.ShapeDtypeStruct((here, width), F32),
            jax.ShapeDtypeStruct((layers, width, units), F32),
            jax.ShapeDtypeStruct((layers, width, units), F32),
            jax.ShapeDtypeStruct((layers, units, width), F32),
        ),
        in_specs=[smem] * 5 + [vmem] * 7,
        out_specs=(vmem,) * 5,
        scratch_shapes=[
            pltpu.VMEM((here, n_sub * here), BF16),
            pltpu.VMEM((here, n_dom * slots * blk), BF16),
            pltpu.VMEM((layers, here, width), BF16),
            pltpu.VMEM((layers, n_sub, here, width), BF16),
            pltpu.VMEM((layers, here, width), BF16),
            pltpu.VMEM((layers, here, units), F32),
            pltpu.VMEM((layers, here, units), BF16),
            pltpu.VMEM((n_sub, here, width), F32),
            pltpu.VMEM(edge, BF16),
            pltpu.VMEM(edge, BF16),
            pltpu.VMEM(edge, BF16),
            pltpu.VMEM(edge, BF16),
            pltpu.VMEM((layers, n_sub + 1, here, width), BF16),
            pltpu.VMEM(tall, BF16),
            pltpu.VMEM(tall, BF16),
            pltpu.VMEM(tall, BF16),
            pltpu.VMEM(small, BF16),
            pltpu.VMEM(small, BF16),
            pltpu.VMEM(small, BF16),
            dma((layers, n_sub, chunks, 2)),
            dma((layers, n_sub, chunks)),
            dma((layers, n_dom)),
            dma((layers, n_dom)),
            dma((layers, n_dom)),
            dma((layers, n_dom)),
            dma((layers, n_sub, chunks)),
            dma((layers, n_sub + 1, chunks)),
            dma((layers, n_dom)),
            dma((layers, n_dom)),
            dma((layers, n_sub)),
            dma((layers, n_sub)),
            dma((layers, n_sub)),
            dma((layers, n_sub)),
            dma((layers, n_dom)),
            dma((layers, n_dom)),
        ],
        compiler_params=pltpu.CompilerParams(
            collective_id=0, has_side_effects=True, vmem_limit_bytes=60 * 1024 * 1024
        ),
    )(local_blocks, remote_blocks, send_blocks, send_counts, partner, features, local_matrix,
      remote_matrix, self_weight, neighbor_weight, output_weight, output_cotangent)


def solution(mesh):
    whole = ("region", "dom", "sub")
    in_specs = (
        P(whole, None), P(whole, None), P(whole, None, None, None), P(whole, None),
        P(whole, None, None, None), P(whole, None, None), P(whole, None), P("region", None),
        P(), P(), P(), P(whole, None),
    )
    out_specs = (
        P(whole, None), P(whole, None), P("region", None, None), P("region", None, None),
        P("region", None, None),
    )
    return jax.shard_map(local, mesh=mesh, in_specs=in_specs, out_specs=out_specs, check_vma=False)
```

```python
import functools

import jax
import jax.numpy as jnp
from jax import lax
from jax.experimental import pallas as pl
from jax.experimental.pallas import tpu as pltpu
from jax.sharding import PartitionSpec as P

F32 = jnp.float32
BF16 = jnp.bfloat16
ROWS = 16


def dot(a, b):
    return jnp.dot(a, b, preferred_element_type=F32)


def dot_nt(a, b):
    return lax.dot_general(a, b, (((1,), (1,)), ((), ())), preferred_element_type=F32)


def dot_tn(a, b):
    return lax.dot_general(a, b, (((0,), (0,)), ((), ())), preferred_element_type=F32)


def kernel(
    n_dom, n_sub,
    lb, rb, sb, sc, pt,
    x_ref, lm_h, rm_h, ws_h, wn_h, wo_h, ct_h,
    upd, fg, wfull,
    lm, rm, ws, wn, wo, ct, in_sem,
    adj, far, st, ag, agg, pre, hid, own,
    bsend, brecv, rsend, rrecv, rs,
    wpart, crecv, xsend, xrecv, zpart, zrecv,
    ag_s, ag_r, bf_s, bf_r, bb_s, bb_r, rs_s, rs_r,
    wc_s, wc_r, wx_s, wx_r, wz_s, wz_r, we_s, we_r, wf_s, wf_r, wm_s, wm_r,
):
    layers = ws.shape[0]
    nb, blk = lm.shape[0], lm.shape[2]
    width = x_ref.shape[1]
    rounds, slots = sb.shape[1], sb.shape[2]
    here = nb * blk
    chunks = ag_r.shape[2]
    crow = here // chunks
    dom = lax.axis_index("dom")
    sub = lax.axis_index("sub")
    pending = []

    def remote(src, dst, send, recv, axis, peer):
        return pltpu.make_async_remote_copy(
            src_ref=src, dst_ref=dst, send_sem=send, recv_sem=recv,
            device_id={axis: peer}, device_id_type=pl.DeviceIdType.MESH,
        )

    def start(copy, cond=None):
        if cond is None:
            copy.start()
        else:
            pl.when(cond)(copy.start)
        pending.append((copy, cond))

    loads = {}
    for i, (name, src, dst) in enumerate((
        ("lm", lm_h, lm), ("rm", rm_h, rm), ("ws", ws_h, ws),
        ("wn", wn_h, wn), ("wo", wo_h, wo), ("ct", ct_h, ct),
    )):
        loads[name] = pltpu.make_async_copy(src, dst, in_sem.at[i])
        loads[name].start()

    barrier = pltpu.get_barrier_semaphore()
    for axis, me, n in (("dom", dom, n_dom), ("sub", sub, n_sub)):
        for d in range(1, n):
            pl.semaphore_signal(
                barrier, inc=1, device_id={axis: lax.rem(me + d, n)},
                device_id_type=pl.DeviceIdType.MESH,
            )
    pl.semaphore_wait(barrier, n_dom + n_sub - 2)

    right, left = jnp.minimum(sub + 1, n_sub - 1), jnp.maximum(sub - 1, 0)
    has_right, has_left = sub < n_sub - 1, sub > 0

    def gather_start(l):
        for c in range(chunks):
            part = st.at[l, pl.ds(c * crow, crow)]
            there = ag.at[l, sub, pl.ds(c * crow, crow)]
            start(remote(part, there, ag_s.at[l, sub, c, 0], ag_r.at[l, sub, c], "sub", right), has_right)
            start(remote(part, there, ag_s.at[l, sub, c, 1], ag_r.at[l, sub, c], "sub", left), has_left)

    def gather_step(l, d, c):
        for _ in (0,):
            for src, ok, to, more, way in (
                (sub - d, sub - d >= 0, right, has_right, 0),
                (sub + d, sub + d < n_sub, left, has_left, 1),
            ):
                at = jnp.clip(src, 0, n_sub - 1)
                part = ag.at[l, at, pl.ds(c * crow, crow)]
                copy = remote(part, part, ag_s.at[l, at, c, way], ag_r.at[l, at, c], "sub", to)
                pl.when(ok)(copy.wait_recv)
                start(copy, jnp.logical_and(ok, more))

    def picks(p, j):
        out = []
        for b in range(nb):
            one = jnp.float32(0.0)
            for r in range(rounds):
                good = (pt[r, dom] == p) & (j < sc[0, r]) & (sb[0, r, j] == b)
                one = one + jnp.where(good, 1.0, 0.0)
            out.append(one)
        return out

    def boundary_start(l):
        for d in range(1, n_dom):
            p = lax.rem(dom + d, n_dom)
            for j in range(slots):
                ones = picks(p, j)
                total = jnp.zeros((blk, width), F32)
                for b in range(nb):
                    total = total + st[l, b * blk:(b + 1) * blk, :].astype(F32) * ones[b]
                bsend[l, p, j * blk:(j + 1) * blk, :] = total.astype(BF16)
            start(remote(bsend.at[l, p], brecv.at[l, dom], bf_s.at[l, p], bf_r.at[l, dom], "dom", p))

    def arrive(buf, sems, l, axis, me, n):
        for d in range(1, n):
            src = lax.rem(me + n - d, n)
            remote(buf.at[l, src], buf.at[l, src], sems.at[l, src], sems.at[l, src], axis, src).wait_recv()

    def build(matrix, column, out, low, count):
        @pl.loop(low, count)
        def _(t):
            at = pl.multiple_of(t * blk, blk)
            for b in range(nb):
                total = jnp.zeros((blk, blk), F32)
                for k in range(matrix.shape[1]):
                    hit = jnp.where(column(b, k) == t, 1.0, 0.0)
                    total = total + matrix[b, k].astype(F32) * hit
                out[b * blk:(b + 1) * blk, pl.ds(at, blk)] = total.astype(BF16)

    def far_column(b, k):
        slot = rb[b, k]
        r = lax.div(slot, slots)
        return pt[r, dom] * slots + (slot - r * slots)

    def local_column(b, k):
        return lb[b, k]

    def gathered(l, d):
        for raw in (sub - d, sub + d):
            @pl.when(jnp.logical_and(raw >= 0, raw < n_sub))
            def _(at=jnp.clip(raw, 0, n_sub - 1)):
                cols = pl.ds(pl.multiple_of(at * here, here), here)
                own[0] += dot(adj[:, cols], ag[l, at])

    st[0] = x_ref[...]
    for l in range(layers):
        gather_start(l)
        boundary_start(l)
        brecv[l, dom] = jnp.zeros(brecv.shape[2:], BF16)
        if l == 0:
            half = n_sub * nb // 2
            loads["lm"].wait()
            build(lm, local_column, adj, 0, half)
            gather_step(l, 1, 0)
            build(lm, local_column, adj, half, 2 * half)
            for c in range(1, chunks):
                gather_step(l, 1, c)
            loads["rm"].wait()
            build(rm, far_column, far, 0, n_dom * slots)
            loads["ws"].wait()
            pre[l] = dot(st[l], ws[l])
        else:
            pre[l] = dot(st[l], ws[l])
            for c in range(chunks):
                gather_step(l, 1, c)
        own[0] = dot(adj[:, pl.ds(pl.multiple_of(sub * here, here), here)], st[l])
        for d in range(2, n_sub):
            for c in range(chunks):
                gather_step(l, d, c)
                if c == 0:
                    gathered(l, d - 1)
            if d == 2:
                arrive(brecv, bf_r, l, "dom", dom, n_dom)
                own[0] += dot(far[...], brecv[l].reshape(-1, width))
        gathered(l, n_sub - 1)
        if l == 0:
            loads["wn"].wait()
            loads["wo"].wait()
            loads["ct"].wait()
        agg[l] = own[0].astype(BF16)
        preact = pre[l] + dot(agg[l], wn[l])
        pre[l] = preact
        hid[l] = (preact / (1.0 + jnp.exp(-preact))).astype(BF16)
        result = (st[l].astype(F32) + dot(hid[l], wo[l])).astype(BF16)
        if l + 1 < layers:
            st[l + 1] = result
        else:
            upd[...] = result

    wrows = xsend.shape[2]
    zrows = zpart.shape[2]
    pairs = n_dom // 2
    pair, side = lax.div(dom, 2), lax.rem(dom, 2)
    mate = dom + 1 - 2 * side

    def weights_start(l, cot, gp):
        out = dot_tn(hid[l], cot)
        tall = jnp.concatenate(
            [dot_tn(st[l], gp), dot_tn(agg[l], gp),
             jnp.concatenate([out[i:i + width] for i in range(0, out.shape[0], width)], axis=1)],
            axis=0,
        )
        for p in range(n_dom):
            wpart[l, p % 2, p // 2] = tall[p * wrows:(p + 1) * wrows]
        start(remote(wpart.at[l, 1 - side], crecv.at[l], wc_s.at[l], wc_r.at[l], "dom", mate))

    def weights_pair(l):
        remote(crecv.at[l], crecv.at[l], wc_s.at[l], wc_r.at[l], "dom", mate).wait_recv()
        for d in range(1, pairs):
            q = lax.rem(pair + d, pairs)
            xsend[l, q] = (wpart[l, side, q] + crecv[l, q]).astype(BF16)
            start(remote(xsend.at[l, q], xrecv.at[l, pair], wx_s.at[l, q], wx_r.at[l, pair], "dom", 2 * q + side))

    def weights_dom(l):
        total = wpart[l, side, pair] + crecv[l, pair]
        for d in range(1, pairs):
            q = lax.rem(pair + pairs - d, pairs)
            remote(xrecv.at[l, q], xrecv.at[l, q], wx_s.at[l, q], wx_r.at[l, q], "dom", mate).wait_recv()
            total = total + xrecv[l, q].astype(F32)
        total = total.astype(BF16)
        for s in range(n_sub):
            low, high = min(s * zrows, wrows), min((s + 1) * zrows, wrows)
            if high > low:
                zpart[l, s, :high - low] = total[low:high]
            if high - low < zrows:
                zpart[l, s, high - low:] = jnp.zeros((zrows - high + low, total.shape[1]), BF16)
        for d in range(1, n_sub):
            s = lax.rem(sub + d, n_sub)
            start(remote(zpart.at[l, s], zrecv.at[l, sub], wz_s.at[l, s], wz_r.at[l, sub], "sub", s))

    def spread(l, s):
        part = wfull.at[l, dom, s]
        start(remote(part, part, wm_s.at[l, pair, s], wm_r.at[l, dom, s], "dom", mate))
        for d in range(1, pairs):
            q = lax.rem(pair + d, pairs)
            start(remote(part, part, wf_s.at[l, q, s], wf_r.at[l, pair, s], "dom", 2 * q + side))

    def weights_sub(l):
        arrive(zrecv, wz_r, l, "sub", sub, n_sub)
        total = zpart[l, sub].astype(F32)
        for d in range(1, n_sub):
            total = total + zrecv[l, lax.rem(sub + d, n_sub)].astype(F32)
        wfull[l, dom, sub] = total.astype(BF16)
        part = wfull.at[l, dom, sub]
        for d in range(1, n_sub):
            s = lax.rem(sub + d, n_sub)
            start(remote(part, part, we_s.at[l, s], we_r.at[l, sub], "sub", s))
        spread(l, sub)

    def weights_back(l):
        for d in range(1, n_sub):
            s = lax.rem(sub + n_sub - d, n_sub)
            part = wfull.at[l, dom, s]
            remote(part, part, we_s.at[l, s], we_r.at[l, s], "sub", s).wait_recv()
            spread(l, s)

    def weights_pass(l):
        for k in range(n_sub):
            s = lax.rem(sub + n_sub - k, n_sub)
            for d in range(1, pairs):
                q = lax.rem(pair + pairs - d, pairs)
                part = wfull.at[l, 2 * q + side, s]
                remote(part, part, wf_s.at[l, q, s], wf_r.at[l, q, s], "dom", mate).wait_recv()
                start(remote(part, part, wm_s.at[l, q, s], wm_r.at[l, 2 * q + side, s], "dom", mate))

    def weights_done(l):
        for s in range(n_sub):
            for q in range(pairs):
                p = 2 * q + 1 - side
                part = wfull.at[l, p, s]
                remote(part, part, wm_s.at[l, q, s], wm_r.at[l, p, s], "dom", mate).wait_recv()

    def reduce_start(l, ga):
        for d in range(n_sub - 1, -1, -1):
            for way in (0, 1) if d else (0,):
                raw = sub - d if way else sub + d
                ok = raw >= 0 if way else raw < n_sub
                t = jnp.clip(raw, 0, n_sub - 1)

                @pl.when(ok)
                def _(t=t):
                    own[t] = dot_tn(adj[:, pl.ds(pl.multiple_of(t * here, here), here)], ga)

                if d:
                    edge = sub == (n_sub - 1 if way else 0)
                    reduce_send(l, t, way, jnp.logical_and(ok, edge), False)

    def reduce_send(l, t, way, cond, add):
        to = left if way else right
        for c in range(chunks):
            rows = pl.ds(c * crow, crow)
            part = rs.at[l, t, rows]
            land = jnp.where(t == to, n_sub, t) if way else t
            copy = remote(part, rs.at[l, land, rows], rs_s.at[l, t, c], rs_r.at[l, land, c], "sub", to)

            @pl.when(cond)
            def _(t=t, rows=rows, part=part, c=c):
                value = own[t, rows]
                if add:
                    remote(part, part, rs_s.at[l, t, c], rs_r.at[l, t, c], "sub", to).wait_recv()
                    value = value + rs[l, t, rows].astype(F32)
                rs[l, t, rows] = value.astype(BF16)

            start(copy, cond)

    def reduce_finish(l):
        for d in range(n_sub - 1, 0, -1):
            for way in (0, 1):
                raw = sub - d if way else sub + d
                ok = raw >= 0 if way else raw < n_sub
                inner = has_right if way else has_left
                reduce_send(l, jnp.clip(raw, 0, n_sub - 1), way, jnp.logical_and(ok, inner), True)

    def reduce_last(l):
        for cond, slot in ((has_left, sub), (has_right, n_sub)):
            @pl.when(cond)
            def _(slot=slot):
                for c in range(chunks):
                    rows = pl.ds(c * crow, crow)
                    part = rs.at[l, slot, rows]
                    remote(part, part, rs_r.at[l, slot, c], rs_r.at[l, slot, c], "sub", left).wait_recv()
                    own[sub, rows] += rs[l, slot, rows].astype(F32)
        return own[sub]

    fg[...] = ct[...].astype(F32)
    for l in range(layers - 1, -1, -1):
        cot = fg[...].astype(BF16)
        preact = pre[l]
        logistic = 1.0 / (1.0 + jnp.exp(-preact))
        gp = (dot_nt(cot, wo[l]) * logistic * (1.0 + preact * (1.0 - logistic))).astype(BF16)
        ga = dot_nt(gp, wn[l]).astype(BF16)
        reduce_start(l, ga)
        rsend[l] = dot_tn(far[...], ga).astype(BF16).reshape(rsend.shape[1:])
        for d in range(1, n_dom):
            p = lax.rem(dom + d, n_dom)
            start(remote(rsend.at[l, p], rrecv.at[l, dom], bb_s.at[l, p], bb_r.at[l, dom], "dom", p))
        weights_start(l, cot, gp)
        if l + 1 < layers:
            weights_sub(l + 1)
        upstream = fg[...] + dot_nt(gp, ws[l])
        weights_pair(l)
        reduce_finish(l)
        fg[...] = upstream
        weights_dom(l)
        arrive(rrecv, bb_r, l, "dom", dom, n_dom)
        for d in range(1, n_dom):
            p = lax.rem(dom + d, n_dom)
            for j in range(slots):
                ones = picks(p, j)
                slot = rrecv[l, p, j * blk:(j + 1) * blk, :].astype(F32)
                for b in range(nb):
                    fg[b * blk:(b + 1) * blk, :] += slot * ones[b]
        near = reduce_last(l)
        fg[...] = fg[...] + near
    for l in range(layers - 1, 0, -1):
        weights_back(l)
    weights_sub(0)
    for l in range(layers - 1, 0, -1):
        weights_pass(l)
    weights_back(0)
    weights_pass(0)
    for l in range(layers):
        weights_done(l)
    for copy, cond in pending:
        if cond is None:
            copy.wait_send()
        else:
            pl.when(cond)(copy.wait_send)


def finish(scale, wrows, u_ref, f_ref, w_ref, upd, fg, gs, gn, go):
    upd[...] = u_ref[...]
    fg[...] = f_ref[...]
    n_dom, n_sub, zrows, units = w_ref.shape[1:]
    width = gs.shape[1]
    tall = w_ref[0].reshape(n_dom, n_sub * zrows, units)
    for p in range(n_dom):
        low = p * wrows
        while low < (p + 1) * wrows:
            high = min((p + 1) * wrows, (low // width + 1) * width)
            part = tall[p, low - p * wrows:high - p * wrows].astype(F32) * scale
            at = low % width
            if low < width:
                gs[0, at:at + high - low] = part
            elif low < 2 * width:
                gn[0, at:at + high - low] = part
            else:
                for i in range(0, units, width):
                    go[0, i + at:i + at + high - low] = part[:, i:i + width]
            low = high


def local(features, local_blocks, local_matrix, remote_blocks, remote_matrix, send_blocks,
          send_counts, partner, self_weight, neighbor_weight, output_weight, output_cotangent):
    n_dom, n_sub = lax.axis_size("dom"), lax.axis_size("sub")
    layers, width, units = self_weight.shape
    here = features.shape[0]
    nb, blk = local_matrix.shape[0], local_matrix.shape[2]
    slots = send_blocks.shape[2]
    scale = 1.0 / (here * n_dom * n_sub) ** 0.5
    chunks = 2
    wrows = 3 * width // n_dom
    zrows = -(-wrows // (n_sub * ROWS)) * ROWS
    vmem, smem = pl.BlockSpec(memory_space=pltpu.VMEM), pl.BlockSpec(memory_space=pltpu.SMEM)
    dma = pltpu.SemaphoreType.DMA
    edge = (layers, n_dom, slots * blk, width)
    half = (layers, n_dom // 2, wrows, units)
    small = (layers, n_sub, zrows, units)
    full = (layers, n_dom, n_sub, zrows, units)
    anywhere = pl.BlockSpec(memory_space=pl.ANY)
    upd, fg, weights = pl.pallas_call(
        functools.partial(kernel, n_dom, n_sub),
        out_shape=(
            jax.ShapeDtypeStruct((here, width), BF16),
            jax.ShapeDtypeStruct((here, width), F32),
            jax.ShapeDtypeStruct(full, BF16),
        ),
        in_specs=[smem] * 5 + [vmem] + [anywhere] * 6,
        out_specs=(vmem,) * 3,
        scratch_shapes=[
            pltpu.VMEM(local_matrix.shape, BF16),
            pltpu.VMEM(remote_matrix.shape, BF16),
            pltpu.VMEM(self_weight.shape, BF16),
            pltpu.VMEM(neighbor_weight.shape, BF16),
            pltpu.VMEM(output_weight.shape, BF16),
            pltpu.VMEM(output_cotangent.shape, BF16),
            dma((6,)),
            pltpu.VMEM((here, n_sub * here), BF16),
            pltpu.VMEM((here, n_dom * slots * blk), BF16),
            pltpu.VMEM((layers, here, width), BF16),
            pltpu.VMEM((layers, n_sub, here, width), BF16),
            pltpu.VMEM((layers, here, width), BF16),
            pltpu.VMEM((layers, here, units), F32),
            pltpu.VMEM((layers, here, units), BF16),
            pltpu.VMEM((n_sub, here, width), F32),
            pltpu.VMEM(edge, BF16),
            pltpu.VMEM(edge, BF16),
            pltpu.VMEM(edge, BF16),
            pltpu.VMEM(edge, BF16),
            pltpu.VMEM((layers, n_sub + 1, here, width), BF16),
            pltpu.VMEM((layers, 2, n_dom // 2, wrows, units), F32),
            pltpu.VMEM(half, F32),
            pltpu.VMEM(half, BF16),
            pltpu.VMEM(half, BF16),
            pltpu.VMEM(small, BF16),
            pltpu.VMEM(small, BF16),
            dma((layers, n_sub, chunks, 2)),
            dma((layers, n_sub, chunks)),
            dma((layers, n_dom)),
            dma((layers, n_dom)),
            dma((layers, n_dom)),
            dma((layers, n_dom)),
            dma((layers, n_sub, chunks)),
            dma((layers, n_sub + 1, chunks)),
            dma((layers,)),
            dma((layers,)),
            dma((layers, n_dom // 2)),
            dma((layers, n_dom // 2)),
            dma((layers, n_sub)),
            dma((layers, n_sub)),
            dma((layers, n_sub)),
            dma((layers, n_sub)),
            dma((layers, n_dom // 2, n_sub)),
            dma((layers, n_dom // 2, n_sub)),
            dma((layers, n_dom // 2, n_sub)),
            dma((layers, n_dom, n_sub)),
        ],
        compiler_params=pltpu.CompilerParams(
            collective_id=0, has_side_effects=True, vmem_limit_bytes=60 * 1024 * 1024
        ),
    )(local_blocks, remote_blocks, send_blocks, send_counts, partner, features, local_matrix,
      remote_matrix, self_weight, neighbor_weight, output_weight, output_cotangent)
    piece = here // layers

    def rows(shape):
        return pl.BlockSpec((1,) + shape[1:], lambda i: (i,) + (0,) * (len(shape) - 1))

    wide, long = (layers, width, units), (layers, units, width)
    return pl.pallas_call(
        functools.partial(finish, scale, wrows),
        grid=(layers,),
        out_shape=(
            jax.ShapeDtypeStruct((here, width), BF16),
            jax.ShapeDtypeStruct((here, width), F32),
            jax.ShapeDtypeStruct(wide, F32),
            jax.ShapeDtypeStruct(wide, F32),
            jax.ShapeDtypeStruct(long, F32),
        ),
        in_specs=[pl.BlockSpec((piece, width), lambda i: (i, 0))] * 2 + [rows(full)],
        out_specs=(pl.BlockSpec((piece, width), lambda i: (i, 0)),) * 2 + (rows(wide), rows(wide), rows(long)),
        compiler_params=pltpu.CompilerParams(vmem_limit_bytes=32 * 1024 * 1024),
    )(upd, fg, weights)


def solution(mesh):
    whole = ("region", "dom", "sub")
    in_specs = (
        P(whole, None), P(whole, None), P(whole, None, None, None), P(whole, None),
        P(whole, None, None, None), P(whole, None, None), P(whole, None), P("region", None),
        P(), P(), P(), P(whole, None),
    )
    out_specs = (
        P(whole, None), P(whole, None), P("region", None, None), P("region", None, None),
        P("region", None, None),
    )
    return jax.shard_map(local, mesh=mesh, in_specs=in_specs, out_specs=out_specs, check_vma=False)
```

```python
import functools

import jax
import jax.numpy as jnp
from jax import lax
from jax.experimental import pallas as pl
from jax.experimental.pallas import tpu as pltpu
from jax.sharding import PartitionSpec as P

F32 = jnp.float32
BF16 = jnp.bfloat16
ROWS = 16


def dot(a, b):
    return jnp.dot(a, b, preferred_element_type=F32)


def dot_nt(a, b):
    return lax.dot_general(a, b, (((1,), (1,)), ((), ())), preferred_element_type=F32)


def dot_tn(a, b):
    return lax.dot_general(a, b, (((0,), (0,)), ((), ())), preferred_element_type=F32)


def kernel(
    n_dom, n_sub,
    lb, rb, sb, sc, pt,
    x_ref, lm_h, rm_h, ws_h, wn_h, wo_h, ct_h,
    upd, fg, wfull,
    lm, rm, ws, wn, wo, ct, in_sem,
    adj, far, st, ag, agg, pre, hid, gh, own,
    bsend, brecv, rsend, rrecv, rs,
    wpart, crecv, xsend, xrecv, zpart, zrecv,
    ag_s, ag_r, bf_s, bf_r, bb_s, bb_r, rs_s, rs_r,
    wc_s, wc_r, wx_s, wx_r, wz_s, wz_r, we_s, we_r, wf_s, wf_r, wm_s, wm_r,
):
    layers = ws.shape[0]
    nb, blk = lm.shape[0], lm.shape[2]
    width = x_ref.shape[1]
    rounds, slots = sb.shape[1], sb.shape[2]
    here = nb * blk
    chunks = ag_r.shape[2]
    crow = here // chunks
    dom = lax.axis_index("dom")
    sub = lax.axis_index("sub")
    pending = []

    def remote(src, dst, send, recv, axis, peer):
        return pltpu.make_async_remote_copy(
            src_ref=src, dst_ref=dst, send_sem=send, recv_sem=recv,
            device_id={axis: peer}, device_id_type=pl.DeviceIdType.MESH,
        )

    def start(copy, cond=None):
        if cond is None:
            copy.start()
        else:
            pl.when(cond)(copy.start)
        pending.append((copy, cond))

    loads = {}
    for i, (name, src, dst) in enumerate((
        ("lm", lm_h, lm), ("rm", rm_h, rm), ("ws", ws_h, ws),
        ("wn", wn_h, wn), ("wo", wo_h, wo), ("ct", ct_h, ct),
    )):
        loads[name] = pltpu.make_async_copy(src, dst, in_sem.at[i])
        loads[name].start()

    barrier = pltpu.get_barrier_semaphore()
    for axis, me, n in (("dom", dom, n_dom), ("sub", sub, n_sub)):
        for d in range(1, n):
            pl.semaphore_signal(
                barrier, inc=1, device_id={axis: lax.rem(me + d, n)},
                device_id_type=pl.DeviceIdType.MESH,
            )
    pl.semaphore_wait(barrier, n_dom + n_sub - 2)

    right, left = jnp.minimum(sub + 1, n_sub - 1), jnp.maximum(sub - 1, 0)
    has_right, has_left = sub < n_sub - 1, sub > 0

    def gather_start(l, c):
        for _ in (0,):
            part = st.at[l, pl.ds(c * crow, crow)]
            there = ag.at[l, sub, pl.ds(c * crow, crow)]
            start(remote(part, there, ag_s.at[l, sub, c, 0], ag_r.at[l, sub, c], "sub", right), has_right)
            start(remote(part, there, ag_s.at[l, sub, c, 1], ag_r.at[l, sub, c], "sub", left), has_left)

    def gather_step(l, d, c):
        for _ in (0,):
            for src, ok, to, more, way in (
                (sub - d, sub - d >= 0, right, has_right, 0),
                (sub + d, sub + d < n_sub, left, has_left, 1),
            ):
                at = jnp.clip(src, 0, n_sub - 1)
                part = ag.at[l, at, pl.ds(c * crow, crow)]
                copy = remote(part, part, ag_s.at[l, at, c, way], ag_r.at[l, at, c], "sub", to)
                pl.when(ok)(copy.wait_recv)
                start(copy, jnp.logical_and(ok, more))

    def picks(p, j):
        out = []
        for b in range(nb):
            one = jnp.float32(0.0)
            for r in range(rounds):
                good = (pt[r, dom] == p) & (j < sc[0, r]) & (sb[0, r, j] == b)
                one = one + jnp.where(good, 1.0, 0.0)
            out.append(one)
        return out

    def boundary_start(l):
        for d in range(1, n_dom):
            p = lax.rem(dom + d, n_dom)
            for j in range(slots):
                ones = picks(p, j)
                total = jnp.zeros((blk, width), F32)
                for b in range(nb):
                    total = total + st[l, b * blk:(b + 1) * blk, :].astype(F32) * ones[b]
                bsend[l, p, j * blk:(j + 1) * blk, :] = total.astype(BF16)
            start(remote(bsend.at[l, p], brecv.at[l, dom], bf_s.at[l, p], bf_r.at[l, dom], "dom", p))

    def arrive(buf, sems, l, axis, me, n):
        for d in range(1, n):
            src = lax.rem(me + n - d, n)
            remote(buf.at[l, src], buf.at[l, src], sems.at[l, src], sems.at[l, src], axis, src).wait_recv()

    def build(matrix, column, out, low, count):
        @pl.loop(low, count)
        def _(t):
            at = pl.multiple_of(t * blk, blk)
            for b in range(nb):
                total = jnp.zeros((blk, blk), F32)
                for k in range(matrix.shape[1]):
                    hit = jnp.where(column(b, k) == t, 1.0, 0.0)
                    total = total + matrix[b, k].astype(F32) * hit
                out[b * blk:(b + 1) * blk, pl.ds(at, blk)] = total.astype(BF16)

    def far_column(b, k):
        slot = rb[b, k]
        r = lax.div(slot, slots)
        return pt[r, dom] * slots + (slot - r * slots)

    def local_column(b, k):
        return lb[b, k]

    def gathered(l, d):
        for raw in (sub - d, sub + d):
            @pl.when(jnp.logical_and(raw >= 0, raw < n_sub))
            def _(at=jnp.clip(raw, 0, n_sub - 1)):
                cols = pl.ds(pl.multiple_of(at * here, here), here)
                fg[...] += dot(adj[:, cols], ag[l, at])

    st[0] = x_ref[...]
    for l in range(layers):
        if l == 0:
            for c in range(chunks):
                gather_start(l, c)
        boundary_start(l)
        brecv[l, dom] = jnp.zeros(brecv.shape[2:], BF16)
        if l == 0:
            half = n_sub * nb // 2
            loads["lm"].wait()
            build(lm, local_column, adj, 0, half)
            gather_step(l, 1, 0)
            build(lm, local_column, adj, half, 2 * half)
            for c in range(1, chunks):
                gather_step(l, 1, c)
            loads["rm"].wait()
            build(rm, far_column, far, 0, n_dom * slots)
            for name in ("ws", "wn", "wo", "ct"):
                loads[name].wait()
            pre[l] = dot(st[l], ws[l])
        else:
            pre[l] = dot(st[l], ws[l])
            for c in range(chunks):
                gather_step(l, 1, c)
        fg[...] = dot(adj[:, pl.ds(pl.multiple_of(sub * here, here), here)], st[l])
        for d in range(2, n_sub):
            for c in range(chunks):
                gather_step(l, d, c)
                if c == 0:
                    gathered(l, d - 1)
                    if l == layers - 1 and d == 2:
                        gh[...] = dot_nt(ct[...], wo[l])
            if d == 2:
                arrive(brecv, bf_r, l, "dom", dom, n_dom)
                fg[...] += dot(far[...], brecv[l].reshape(-1, width))
        gathered(l, n_sub - 1)
        for c in range(chunks):
            rows = slice(c * crow, (c + 1) * crow)
            agg[l, rows] = fg[rows].astype(BF16)
            preact = pre[l, rows] + dot(agg[l, rows], wn[l])
            pre[l, rows] = preact
            hid[l, rows] = (preact / (1.0 + jnp.exp(-preact))).astype(BF16)
            result = (st[l, rows].astype(F32) + dot(hid[l, rows], wo[l])).astype(BF16)
            if l + 1 < layers:
                st[l + 1, rows] = result
                gather_start(l + 1, c)
            else:
                upd[rows] = result

    wrows = xsend.shape[2]
    zrows = zpart.shape[2]
    pairs = n_dom // 2
    pair, side = lax.div(dom, 2), lax.rem(dom, 2)
    mate = dom + 1 - 2 * side

    def weights_start(l, cot, gp):
        out = dot_tn(hid[l], cot)
        tall = jnp.concatenate(
            [dot_tn(st[l], gp), dot_tn(agg[l], gp),
             jnp.concatenate([out[i:i + width] for i in range(0, out.shape[0], width)], axis=1)],
            axis=0,
        )
        for p in range(n_dom):
            wpart[l, p % 2, p // 2] = tall[p * wrows:(p + 1) * wrows]
        start(remote(wpart.at[l, 1 - side], crecv.at[l], wc_s.at[l], wc_r.at[l], "dom", mate))

    def weights_pair(l):
        remote(crecv.at[l], crecv.at[l], wc_s.at[l], wc_r.at[l], "dom", mate).wait_recv()
        for d in range(1, pairs):
            q = lax.rem(pair + d, pairs)
            xsend[l, q] = (wpart[l, side, q] + crecv[l, q]).astype(BF16)
            start(remote(xsend.at[l, q], xrecv.at[l, pair], wx_s.at[l, q], wx_r.at[l, pair], "dom", 2 * q + side))

    def weights_dom(l):
        total = wpart[l, side, pair] + crecv[l, pair]
        for d in range(1, pairs):
            q = lax.rem(pair + pairs - d, pairs)
            remote(xrecv.at[l, q], xrecv.at[l, q], wx_s.at[l, q], wx_r.at[l, q], "dom", mate).wait_recv()
            total = total + xrecv[l, q].astype(F32)
        total = total.astype(BF16)
        for s in range(n_sub):
            low, high = min(s * zrows, wrows), min((s + 1) * zrows, wrows)
            if high > low:
                zpart[l, s, :high - low] = total[low:high]
            if high - low < zrows:
                zpart[l, s, high - low:] = jnp.zeros((zrows - high + low, total.shape[1]), BF16)
        for d in range(1, n_sub):
            s = lax.rem(sub + d, n_sub)
            start(remote(zpart.at[l, s], zrecv.at[l, sub], wz_s.at[l, s], wz_r.at[l, sub], "sub", s))

    def spread(l, s):
        part = wfull.at[l, dom, s]
        start(remote(part, part, wm_s.at[l, pair, s], wm_r.at[l, dom, s], "dom", mate))
        for d in range(1, pairs):
            q = lax.rem(pair + d, pairs)
            start(remote(part, part, wf_s.at[l, q, s], wf_r.at[l, pair, s], "dom", 2 * q + side))

    def weights_sub(l):
        arrive(zrecv, wz_r, l, "sub", sub, n_sub)
        total = zpart[l, sub].astype(F32)
        for d in range(1, n_sub):
            total = total + zrecv[l, lax.rem(sub + d, n_sub)].astype(F32)
        wfull[l, dom, sub] = total.astype(BF16)
        part = wfull.at[l, dom, sub]
        for d in range(1, n_sub):
            s = lax.rem(sub + d, n_sub)
            start(remote(part, part, we_s.at[l, s], we_r.at[l, sub], "sub", s))
        spread(l, sub)

    def weights_back(l):
        for d in range(1, n_sub):
            s = lax.rem(sub + n_sub - d, n_sub)
            part = wfull.at[l, dom, s]
            remote(part, part, we_s.at[l, s], we_r.at[l, s], "sub", s).wait_recv()
            spread(l, s)

    def weights_pass(l):
        for k in range(n_sub):
            s = lax.rem(sub + n_sub - k, n_sub)
            for d in range(1, pairs):
                q = lax.rem(pair + pairs - d, pairs)
                part = wfull.at[l, 2 * q + side, s]
                remote(part, part, wf_s.at[l, q, s], wf_r.at[l, q, s], "dom", mate).wait_recv()
                start(remote(part, part, wm_s.at[l, q, s], wm_r.at[l, 2 * q + side, s], "dom", mate))

    def weights_done(l):
        for s in range(n_sub):
            for q in range(pairs):
                p = 2 * q + 1 - side
                part = wfull.at[l, p, s]
                remote(part, part, wm_s.at[l, q, s], wm_r.at[l, p, s], "dom", mate).wait_recv()

    trow = width // chunks
    def reduce_start(l, ga):
        for d in range(n_sub - 1, -1, -1):
            for way in (0, 1) if d else (0,):
                raw = sub - d if way else sub + d
                ok = raw >= 0 if way else raw < n_sub
                t = jnp.clip(raw, 0, n_sub - 1)

                @pl.when(ok)
                def _(t=t):
                    own[t] = dot(ga, adj[:, pl.ds(pl.multiple_of(t * here, here), here)])

                if d:
                    edge = sub == (n_sub - 1 if way else 0)
                    reduce_send(l, t, way, jnp.logical_and(ok, edge), False)

    def reduce_send(l, t, way, cond, add):
        to = left if way else right
        for c in range(chunks):
            rows = pl.ds(c * trow, trow)
            part = rs.at[l, t, rows]
            land = jnp.where(t == to, n_sub, t) if way else t
            copy = remote(part, rs.at[l, land, rows], rs_s.at[l, t, c], rs_r.at[l, land, c], "sub", to)

            @pl.when(cond)
            def _(t=t, rows=rows, part=part, c=c):
                value = own[t, rows]
                if add:
                    remote(part, part, rs_s.at[l, t, c], rs_r.at[l, t, c], "sub", to).wait_recv()
                    value = value + rs[l, t, rows].astype(F32)
                rs[l, t, rows] = value.astype(BF16)

            start(copy, cond)

    def reduce_finish(l):
        for d in range(n_sub - 1, 0, -1):
            for way in (0, 1):
                raw = sub - d if way else sub + d
                ok = raw >= 0 if way else raw < n_sub
                inner = has_right if way else has_left
                reduce_send(l, jnp.clip(raw, 0, n_sub - 1), way, jnp.logical_and(ok, inner), True)

    def reduce_last(l):
        for cond, slot in ((has_left, sub), (has_right, n_sub)):
            @pl.when(cond)
            def _(slot=slot):
                for c in range(chunks):
                    rows = pl.ds(c * trow, trow)
                    part = rs.at[l, slot, rows]
                    remote(part, part, rs_r.at[l, slot, c], rs_r.at[l, slot, c], "sub", left).wait_recv()
                    own[sub, rows] += rs[l, slot, rows].astype(F32)

    fg[...] = ct[...].astype(F32)
    for l in range(layers - 1, -1, -1):
        cot = fg[...].astype(BF16)
        preact = pre[l]
        logistic = 1.0 / (1.0 + jnp.exp(-preact))
        above = gh[...] if l == layers - 1 else dot_nt(cot, wo[l])
        gp = (above * logistic * (1.0 + preact * (1.0 - logistic))).astype(BF16)
        ga = dot_nt(wn[l], gp).astype(BF16)
        reduce_start(l, ga)
        for d in range(1, n_dom):
            p = lax.rem(dom + d, n_dom)
            cols = pl.ds(pl.multiple_of(p * slots * blk, slots * blk), slots * blk)
            rsend[l, p] = dot(ga, far[:, cols]).astype(BF16)
            start(remote(rsend.at[l, p], rrecv.at[l, dom], bb_s.at[l, p], bb_r.at[l, dom], "dom", p))
        weights_start(l, cot, gp)
        if l + 1 < layers:
            weights_sub(l + 1)
        upstream = fg[...] + dot_nt(gp, ws[l])
        weights_pair(l)
        reduce_finish(l)
        fg[...] = upstream
        weights_dom(l)
        arrive(rrecv, bb_r, l, "dom", dom, n_dom)
        for d in range(1, n_dom):
            p = lax.rem(dom + d, n_dom)
            for j in range(slots):
                ones = picks(p, j)
                slot = rrecv[l, p, :, j * blk:(j + 1) * blk].astype(F32)
                for b in range(nb):
                    own[sub, :, b * blk:(b + 1) * blk] += slot * ones[b]
        reduce_last(l)
        fg[...] += own[sub].T
    for l in range(layers - 1, 0, -1):
        weights_back(l)
    weights_sub(0)
    for l in range(layers - 1, 0, -1):
        weights_pass(l)
    weights_back(0)
    weights_pass(0)
    for l in range(layers):
        weights_done(l)
    for copy, cond in pending:
        if cond is None:
            copy.wait_send()
        else:
            pl.when(cond)(copy.wait_send)


def finish(scale, wrows, u_ref, f_ref, w_ref, upd, fg, gs, gn, go):
    upd[...] = u_ref[...]
    fg[...] = f_ref[...]
    n_dom, n_sub, zrows, units = w_ref.shape[1:]
    width = gs.shape[1]
    tall = w_ref[0].reshape(n_dom, n_sub * zrows, units)
    for p in range(n_dom):
        low = p * wrows
        while low < (p + 1) * wrows:
            high = min((p + 1) * wrows, (low // width + 1) * width)
            part = tall[p, low - p * wrows:high - p * wrows].astype(F32) * scale
            at = low % width
            if low < width:
                gs[0, at:at + high - low] = part
            elif low < 2 * width:
                gn[0, at:at + high - low] = part
            else:
                for i in range(0, units, width):
                    go[0, i + at:i + at + high - low] = part[:, i:i + width]
            low = high


def local(features, local_blocks, local_matrix, remote_blocks, remote_matrix, send_blocks,
          send_counts, partner, self_weight, neighbor_weight, output_weight, output_cotangent):
    n_dom, n_sub = lax.axis_size("dom"), lax.axis_size("sub")
    layers, width, units = self_weight.shape
    here = features.shape[0]
    nb, blk = local_matrix.shape[0], local_matrix.shape[2]
    slots = send_blocks.shape[2]
    scale = 1.0 / (here * n_dom * n_sub) ** 0.5
    chunks = 2
    wrows = 3 * width // n_dom
    zrows = -(-wrows // (n_sub * ROWS)) * ROWS
    vmem, smem = pl.BlockSpec(memory_space=pltpu.VMEM), pl.BlockSpec(memory_space=pltpu.SMEM)
    dma = pltpu.SemaphoreType.DMA
    edge = (layers, n_dom, slots * blk, width)
    back = (layers, n_dom, width, slots * blk)
    half = (layers, n_dom // 2, wrows, units)
    small = (layers, n_sub, zrows, units)
    full = (layers, n_dom, n_sub, zrows, units)
    anywhere = pl.BlockSpec(memory_space=pl.ANY)
    upd, fg, weights = pl.pallas_call(
        functools.partial(kernel, n_dom, n_sub),
        out_shape=(
            jax.ShapeDtypeStruct((here, width), BF16),
            jax.ShapeDtypeStruct((here, width), F32),
            jax.ShapeDtypeStruct(full, BF16),
        ),
        in_specs=[smem] * 5 + [vmem] + [anywhere] * 6,
        out_specs=(vmem,) * 3,
        scratch_shapes=[
            pltpu.VMEM(local_matrix.shape, BF16),
            pltpu.VMEM(remote_matrix.shape, BF16),
            pltpu.VMEM(self_weight.shape, BF16),
            pltpu.VMEM(neighbor_weight.shape, BF16),
            pltpu.VMEM(output_weight.shape, BF16),
            pltpu.VMEM(output_cotangent.shape, BF16),
            dma((6,)),
            pltpu.VMEM((here, n_sub * here), BF16),
            pltpu.VMEM((here, n_dom * slots * blk), BF16),
            pltpu.VMEM((layers, here, width), BF16),
            pltpu.VMEM((layers, n_sub, here, width), BF16),
            pltpu.VMEM((layers, here, width), BF16),
            pltpu.VMEM((layers, here, units), F32),
            pltpu.VMEM((layers, here, units), BF16),
            pltpu.VMEM((here, units), F32),
            pltpu.VMEM((n_sub, width, here), F32),
            pltpu.VMEM(edge, BF16),
            pltpu.VMEM(edge, BF16),
            pltpu.VMEM(back, BF16),
            pltpu.VMEM(back, BF16),
            pltpu.VMEM((layers, n_sub + 1, width, here), BF16),
            pltpu.VMEM((layers, 2, n_dom // 2, wrows, units), F32),
            pltpu.VMEM(half, F32),
            pltpu.VMEM(half, BF16),
            pltpu.VMEM(half, BF16),
            pltpu.VMEM(small, BF16),
            pltpu.VMEM(small, BF16),
            dma((layers, n_sub, chunks, 2)),
            dma((layers, n_sub, chunks)),
            dma((layers, n_dom)),
            dma((layers, n_dom)),
            dma((layers, n_dom)),
            dma((layers, n_dom)),
            dma((layers, n_sub, chunks)),
            dma((layers, n_sub + 1, chunks)),
            dma((layers,)),
            dma((layers,)),
            dma((layers, n_dom // 2)),
            dma((layers, n_dom // 2)),
            dma((layers, n_sub)),
            dma((layers, n_sub)),
            dma((layers, n_sub)),
            dma((layers, n_sub)),
            dma((layers, n_dom // 2, n_sub)),
            dma((layers, n_dom // 2, n_sub)),
            dma((layers, n_dom // 2, n_sub)),
            dma((layers, n_dom, n_sub)),
        ],
        compiler_params=pltpu.CompilerParams(
            collective_id=0, has_side_effects=True, vmem_limit_bytes=60 * 1024 * 1024
        ),
    )(local_blocks, remote_blocks, send_blocks, send_counts, partner, features, local_matrix,
      remote_matrix, self_weight, neighbor_weight, output_weight, output_cotangent)
    piece = here // layers

    def rows(shape):
        return pl.BlockSpec((1,) + shape[1:], lambda i: (i,) + (0,) * (len(shape) - 1))

    wide, long = (layers, width, units), (layers, units, width)
    return pl.pallas_call(
        functools.partial(finish, scale, wrows),
        grid=(layers,),
        out_shape=(
            jax.ShapeDtypeStruct((here, width), BF16),
            jax.ShapeDtypeStruct((here, width), F32),
            jax.ShapeDtypeStruct(wide, F32),
            jax.ShapeDtypeStruct(wide, F32),
            jax.ShapeDtypeStruct(long, F32),
        ),
        in_specs=[pl.BlockSpec((piece, width), lambda i: (i, 0))] * 2 + [rows(full)],
        out_specs=(pl.BlockSpec((piece, width), lambda i: (i, 0)),) * 2 + (rows(wide), rows(wide), rows(long)),
        compiler_params=pltpu.CompilerParams(vmem_limit_bytes=60 * 1024 * 1024),
    )(upd, fg, weights)


def solution(mesh):
    whole = ("region", "dom", "sub")
    in_specs = (
        P(whole, None), P(whole, None), P(whole, None, None, None), P(whole, None),
        P(whole, None, None, None), P(whole, None, None), P(whole, None), P("region", None),
        P(), P(), P(), P(whole, None),
    )
    out_specs = (
        P(whole, None), P(whole, None), P("region", None, None), P("region", None, None),
        P("region", None, None),
    )
    return jax.shard_map(local, mesh=mesh, in_specs=in_specs, out_specs=out_specs, check_vma=False)
```

```python
import functools

import jax
import jax.numpy as jnp
from jax import lax
from jax.experimental import pallas as pl
from jax.experimental.pallas import tpu as pltpu
from jax.sharding import PartitionSpec as P

F32 = jnp.float32
BF16 = jnp.bfloat16
ROWS = 16


def dot(a, b):
    return jnp.dot(a, b, preferred_element_type=F32)


def dot_nt(a, b):
    return lax.dot_general(a, b, (((1,), (1,)), ((), ())), preferred_element_type=F32)


def dot_tn(a, b):
    return lax.dot_general(a, b, (((0,), (0,)), ((), ())), preferred_element_type=F32)


def kernel(
    n_dom, n_sub,
    lb, rb, sb, sc, pt,
    x_ref, lm_h, rm_h, ws_h, wn_h, wo_h, ct_h,
    upd, fg, wfull,
    lm, rm, ws, wn, wo, ct, in_sem,
    adj, far, st, ag, agg, pre, hid, gh, own,
    bsend, brecv, rsend, rrecv, rs,
    wpart, crecv, xsend, xrecv, zpart, zrecv,
    ag_s, ag_r, bf_s, bf_r, bb_s, bb_r, rs_s, rs_r,
    wc_s, wc_r, wx_s, wx_r, wz_s, wz_r, we_s, we_r, wf_s, wf_r, wm_s, wm_r,
):
    layers = ws.shape[0]
    nb, blk = lm.shape[0], lm.shape[2]
    width = x_ref.shape[1]
    rounds, slots = sb.shape[1], sb.shape[2]
    here = nb * blk
    chunks = ag_r.shape[2]
    crow = here // chunks
    dom = lax.axis_index("dom")
    sub = lax.axis_index("sub")
    pending = []

    def remote(src, dst, send, recv, axis, peer):
        return pltpu.make_async_remote_copy(
            src_ref=src, dst_ref=dst, send_sem=send, recv_sem=recv,
            device_id={axis: peer}, device_id_type=pl.DeviceIdType.MESH,
        )

    def start(copy, cond=None):
        if cond is None:
            copy.start()
        else:
            pl.when(cond)(copy.start)
        pending.append((copy, cond))

    loads = {}
    for i, (name, src, dst) in enumerate((
        ("lm", lm_h, lm), ("rm", rm_h, rm), ("ws", ws_h, ws),
        ("wn", wn_h, wn), ("wo", wo_h, wo), ("ct", ct_h, ct),
    )):
        loads[name] = pltpu.make_async_copy(src, dst, in_sem.at[i])
        loads[name].start()

    barrier = pltpu.get_barrier_semaphore()
    for axis, me, n in (("dom", dom, n_dom), ("sub", sub, n_sub)):
        for d in range(1, n):
            pl.semaphore_signal(
                barrier, inc=1, device_id={axis: lax.rem(me + d, n)},
                device_id_type=pl.DeviceIdType.MESH,
            )
    pl.semaphore_wait(barrier, n_dom + n_sub - 2)

    right, left = jnp.minimum(sub + 1, n_sub - 1), jnp.maximum(sub - 1, 0)
    has_right, has_left = sub < n_sub - 1, sub > 0

    def gather_start(l, c):
        for _ in (0,):
            part = st.at[l, pl.ds(c * crow, crow)]
            there = ag.at[l, sub, pl.ds(c * crow, crow)]
            start(remote(part, there, ag_s.at[l, sub, c, 0], ag_r.at[l, sub, c], "sub", right), has_right)
            start(remote(part, there, ag_s.at[l, sub, c, 1], ag_r.at[l, sub, c], "sub", left), has_left)

    def gather_step(l, d, c):
        for _ in (0,):
            for src, ok, to, more, way in (
                (sub - d, sub - d >= 0, right, has_right, 0),
                (sub + d, sub + d < n_sub, left, has_left, 1),
            ):
                at = jnp.clip(src, 0, n_sub - 1)
                part = ag.at[l, at, pl.ds(c * crow, crow)]
                copy = remote(part, part, ag_s.at[l, at, c, way], ag_r.at[l, at, c], "sub", to)
                pl.when(ok)(copy.wait_recv)
                start(copy, jnp.logical_and(ok, more))

    def picks(p, j):
        out = []
        for b in range(nb):
            one = jnp.float32(0.0)
            for r in range(rounds):
                good = (pt[r, dom] == p) & (j < sc[0, r]) & (sb[0, r, j] == b)
                one = one + jnp.where(good, 1.0, 0.0)
            out.append(one)
        return out

    def boundary_start(l):
        for d in range(1, n_dom):
            p = lax.rem(dom + d, n_dom)
            for j in range(slots):
                ones = picks(p, j)
                total = jnp.zeros((blk, width), F32)
                for b in range(nb):
                    total = total + st[l, b * blk:(b + 1) * blk, :].astype(F32) * ones[b]
                bsend[l, p, j * blk:(j + 1) * blk, :] = total.astype(BF16)
            start(remote(bsend.at[l, p], brecv.at[l, dom], bf_s.at[l, p], bf_r.at[l, dom], "dom", p))

    def arrive(buf, sems, l, axis, me, n):
        for d in range(1, n):
            src = lax.rem(me + n - d, n)
            remote(buf.at[l, src], buf.at[l, src], sems.at[l, src], sems.at[l, src], axis, src).wait_recv()

    def build(matrix, column, out, low, count):
        @pl.loop(low, count)
        def _(t):
            at = pl.multiple_of(t * blk, blk)
            for b in range(nb):
                total = jnp.zeros((blk, blk), F32)
                for k in range(matrix.shape[1]):
                    hit = jnp.where(column(b, k) == t, 1.0, 0.0)
                    total = total + matrix[b, k].astype(F32) * hit
                out[b * blk:(b + 1) * blk, pl.ds(at, blk)] = total.astype(BF16)

    def far_column(b, k):
        slot = rb[b, k]
        r = lax.div(slot, slots)
        return pt[r, dom] * slots + (slot - r * slots)

    def local_column(b, k):
        return lb[b, k]

    def gathered(l, d):
        for raw in (sub - d, sub + d):
            @pl.when(jnp.logical_and(raw >= 0, raw < n_sub))
            def _(at=jnp.clip(raw, 0, n_sub - 1)):
                cols = pl.ds(pl.multiple_of(at * here, here), here)
                fg[...] += dot(adj[:, cols], ag[l, at])

    st[0] = x_ref[...]
    for l in range(layers):
        if l == 0:
            for c in range(chunks):
                gather_start(l, c)
        boundary_start(l)
        brecv[l, dom] = jnp.zeros(brecv.shape[2:], BF16)
        if l == 0:
            half = n_sub * nb // 2
            loads["lm"].wait()
            build(lm, local_column, adj, 0, half)
            gather_step(l, 1, 0)
            build(lm, local_column, adj, half, 2 * half)
            for c in range(1, chunks):
                gather_step(l, 1, c)
            loads["rm"].wait()
            build(rm, far_column, far, 0, n_dom * slots)
            for name in ("ws", "wn", "wo", "ct"):
                loads[name].wait()
            pre[l] = dot(st[l], ws[l])
        else:
            pre[l] = dot(st[l], ws[l])
            for c in range(chunks):
                gather_step(l, 1, c)
        fg[...] = dot(adj[:, pl.ds(pl.multiple_of(sub * here, here), here)], st[l])
        for d in range(2, n_sub):
            for c in range(chunks):
                gather_step(l, d, c)
                if c == 0:
                    gathered(l, d - 1)
                    if l == layers - 1 and d == 2:
                        gh[...] = dot_nt(ct[...], wo[l])
            if d == 2:
                arrive(brecv, bf_r, l, "dom", dom, n_dom)
                fg[...] += dot(far[...], brecv[l].reshape(-1, width))
        gathered(l, n_sub - 1)
        for c in range(chunks):
            rows = slice(c * crow, (c + 1) * crow)
            agg[l, rows] = fg[rows].astype(BF16)
            preact = pre[l, rows] + dot(agg[l, rows], wn[l])
            pre[l, rows] = preact
            hid[l, rows] = (preact / (1.0 + jnp.exp(-preact))).astype(BF16)
            result = (st[l, rows].astype(F32) + dot(hid[l, rows], wo[l])).astype(BF16)
            if l + 1 < layers:
                st[l + 1, rows] = result
                gather_start(l + 1, c)
            else:
                upd[rows] = result

    wrows = xsend.shape[2]
    zrows = zpart.shape[2]
    pairs = n_dom // 2
    pair, side = lax.div(dom, 2), lax.rem(dom, 2)
    mate = dom + 1 - 2 * side

    def weights_start(l, cot, gp):
        out = dot_tn(hid[l], cot)
        tall = jnp.concatenate(
            [dot_tn(st[l], gp), dot_tn(agg[l], gp),
             jnp.concatenate([out[i:i + width] for i in range(0, out.shape[0], width)], axis=1)],
            axis=0,
        )
        for p in range(n_dom):
            wpart[l, p % 2, p // 2] = tall[p * wrows:(p + 1) * wrows]
        start(remote(wpart.at[l, 1 - side], crecv.at[l], wc_s.at[l], wc_r.at[l], "dom", mate))

    def weights_pair(l):
        remote(crecv.at[l], crecv.at[l], wc_s.at[l], wc_r.at[l], "dom", mate).wait_recv()
        for d in range(1, pairs):
            q = lax.rem(pair + d, pairs)
            xsend[l, q] = (wpart[l, side, q] + crecv[l, q]).astype(BF16)
            start(remote(xsend.at[l, q], xrecv.at[l, pair], wx_s.at[l, q], wx_r.at[l, pair], "dom", 2 * q + side))

    def weights_dom(l):
        total = wpart[l, side, pair] + crecv[l, pair]
        for d in range(1, pairs):
            q = lax.rem(pair + pairs - d, pairs)
            remote(xrecv.at[l, q], xrecv.at[l, q], wx_s.at[l, q], wx_r.at[l, q], "dom", mate).wait_recv()
            total = total + xrecv[l, q].astype(F32)
        total = total.astype(BF16)
        for s in range(n_sub):
            low, high = min(s * zrows, wrows), min((s + 1) * zrows, wrows)
            if high > low:
                zpart[l, s, :high - low] = total[low:high]
            if high - low < zrows:
                zpart[l, s, high - low:] = jnp.zeros((zrows - high + low, total.shape[1]), BF16)
        for d in range(1, n_sub):
            s = lax.rem(sub + d, n_sub)
            start(remote(zpart.at[l, s], zrecv.at[l, sub], wz_s.at[l, s], wz_r.at[l, sub], "sub", s))

    def spread(l, s):
        part = wfull.at[l, dom, s]
        start(remote(part, part, wm_s.at[l, pair, s], wm_r.at[l, dom, s], "dom", mate))
        for d in range(1, pairs):
            q = lax.rem(pair + d, pairs)
            start(remote(part, part, wf_s.at[l, q, s], wf_r.at[l, pair, s], "dom", 2 * q + side))

    def weights_sub(l):
        arrive(zrecv, wz_r, l, "sub", sub, n_sub)
        total = zpart[l, sub].astype(F32)
        for d in range(1, n_sub):
            total = total + zrecv[l, lax.rem(sub + d, n_sub)].astype(F32)
        wfull[l, dom, sub] = total.astype(BF16)
        part = wfull.at[l, dom, sub]
        for d in range(1, n_sub):
            s = lax.rem(sub + d, n_sub)
            start(remote(part, part, we_s.at[l, s], we_r.at[l, sub], "sub", s))
        spread(l, sub)

    def weights_back(l):
        for d in range(1, n_sub):
            s = lax.rem(sub + n_sub - d, n_sub)
            part = wfull.at[l, dom, s]
            remote(part, part, we_s.at[l, s], we_r.at[l, s], "sub", s).wait_recv()
            spread(l, s)

    def weights_pass(l):
        for k in range(n_sub):
            s = lax.rem(sub + n_sub - k, n_sub)
            for d in range(1, pairs):
                q = lax.rem(pair + pairs - d, pairs)
                part = wfull.at[l, 2 * q + side, s]
                remote(part, part, wf_s.at[l, q, s], wf_r.at[l, q, s], "dom", mate).wait_recv()
                start(remote(part, part, wm_s.at[l, q, s], wm_r.at[l, 2 * q + side, s], "dom", mate))

    def weights_done(l):
        for s in range(n_sub):
            for q in range(pairs):
                p = 2 * q + 1 - side
                part = wfull.at[l, p, s]
                remote(part, part, wm_s.at[l, q, s], wm_r.at[l, p, s], "dom", mate).wait_recv()

    trow = width // chunks
    def reduce_start(l, ga):
        for d in range(n_sub - 1, -1, -1):
            for way in (0, 1) if d else (0,):
                raw = sub - d if way else sub + d
                ok = raw >= 0 if way else raw < n_sub
                t = jnp.clip(raw, 0, n_sub - 1)

                @pl.when(ok)
                def _(t=t):
                    own[t] = dot(ga, adj[:, pl.ds(pl.multiple_of(t * here, here), here)])

                if d:
                    edge = sub == (n_sub - 1 if way else 0)
                    reduce_send(l, t, way, jnp.logical_and(ok, edge), False)

    def reduce_send(l, t, way, cond, add):
        to = left if way else right
        for c in range(chunks):
            rows = pl.ds(c * trow, trow)
            part = rs.at[l, t, rows]
            land = jnp.where(t == to, n_sub, t) if way else t
            copy = remote(part, rs.at[l, land, rows], rs_s.at[l, t, c], rs_r.at[l, land, c], "sub", to)

            @pl.when(cond)
            def _(t=t, rows=rows, part=part, c=c):
                value = own[t, rows]
                if add:
                    remote(part, part, rs_s.at[l, t, c], rs_r.at[l, t, c], "sub", to).wait_recv()
                    value = value + rs[l, t, rows].astype(F32)
                rs[l, t, rows] = value.astype(BF16)

            start(copy, cond)

    def reduce_finish(l, last, first):
        for d in range(last, first - 1, -1):
            for way in (0, 1):
                raw = sub - d if way else sub + d
                ok = raw >= 0 if way else raw < n_sub
                inner = has_right if way else has_left
                reduce_send(l, jnp.clip(raw, 0, n_sub - 1), way, jnp.logical_and(ok, inner), True)

    def reduce_last(l):
        for cond, slot in ((has_left, sub), (has_right, n_sub)):
            @pl.when(cond)
            def _(slot=slot):
                for c in range(chunks):
                    rows = pl.ds(c * trow, trow)
                    part = rs.at[l, slot, rows]
                    remote(part, part, rs_r.at[l, slot, c], rs_r.at[l, slot, c], "sub", left).wait_recv()
                    own[sub, rows] += rs[l, slot, rows].astype(F32)

    fg[...] = ct[...].astype(F32)
    for l in range(layers - 1, -1, -1):
        cot = fg[...].astype(BF16)
        preact = pre[l]
        logistic = 1.0 / (1.0 + jnp.exp(-preact))
        above = gh[...] if l == layers - 1 else dot_nt(cot, wo[l])
        gp = (above * logistic * (1.0 + preact * (1.0 - logistic))).astype(BF16)
        ga = dot_nt(wn[l], gp).astype(BF16)
        reduce_start(l, ga)
        for d in range(1, n_dom):
            p = lax.rem(dom + d, n_dom)
            cols = pl.ds(pl.multiple_of(p * slots * blk, slots * blk), slots * blk)
            rsend[l, p] = dot(ga, far[:, cols]).astype(BF16)
            start(remote(rsend.at[l, p], rrecv.at[l, dom], bb_s.at[l, p], bb_r.at[l, dom], "dom", p))
        weights_start(l, cot, gp)
        if l + 1 < layers:
            weights_sub(l + 1)
        upstream = fg[...] + dot_nt(gp, ws[l])
        weights_pair(l)
        reduce_finish(l, n_sub - 1, 2)
        if l == 0:
            weights_dom(l)
        reduce_finish(l, 1, 1)
        fg[...] = upstream
        if l == 0:
            weights_sub(l)
            for k in range(layers - 1, 0, -1):
                weights_back(k)
        arrive(rrecv, bb_r, l, "dom", dom, n_dom)
        for d in range(1, n_dom):
            p = lax.rem(dom + d, n_dom)
            for j in range(slots):
                ones = picks(p, j)
                slot = rrecv[l, p, :, j * blk:(j + 1) * blk].astype(F32)
                for b in range(nb):
                    own[sub, :, b * blk:(b + 1) * blk] += slot * ones[b]
        if l == 0:
            weights_back(l)
            for k in range(layers - 1, 0, -1):
                weights_pass(k)
        reduce_last(l)
        if l > 0:
            weights_dom(l)
        fg[...] += own[sub].T
    weights_pass(0)
    for l in range(layers):
        weights_done(l)
    for copy, cond in pending:
        if cond is None:
            copy.wait_send()
        else:
            pl.when(cond)(copy.wait_send)


def finish(scale, wrows, u_ref, f_ref, w_ref, upd, fg, gs, gn, go):
    upd[...] = u_ref[...]
    fg[...] = f_ref[...]
    n_dom, n_sub, zrows, units = w_ref.shape[1:]
    width = gs.shape[1]
    tall = w_ref[0].reshape(n_dom, n_sub * zrows, units)
    for p in range(n_dom):
        low = p * wrows
        while low < (p + 1) * wrows:
            high = min((p + 1) * wrows, (low // width + 1) * width)
            part = tall[p, low - p * wrows:high - p * wrows].astype(F32) * scale
            at = low % width
            if low < width:
                gs[0, at:at + high - low] = part
            elif low < 2 * width:
                gn[0, at:at + high - low] = part
            else:
                for i in range(0, units, width):
                    go[0, i + at:i + at + high - low] = part[:, i:i + width]
            low = high


def local(features, local_blocks, local_matrix, remote_blocks, remote_matrix, send_blocks,
          send_counts, partner, self_weight, neighbor_weight, output_weight, output_cotangent):
    n_dom, n_sub = lax.axis_size("dom"), lax.axis_size("sub")
    layers, width, units = self_weight.shape
    here = features.shape[0]
    nb, blk = local_matrix.shape[0], local_matrix.shape[2]
    slots = send_blocks.shape[2]
    scale = 1.0 / (here * n_dom * n_sub) ** 0.5
    chunks = 2
    wrows = 3 * width // n_dom
    zrows = -(-wrows // (n_sub * ROWS)) * ROWS
    vmem, smem = pl.BlockSpec(memory_space=pltpu.VMEM), pl.BlockSpec(memory_space=pltpu.SMEM)
    dma = pltpu.SemaphoreType.DMA
    edge = (layers, n_dom, slots * blk, width)
    back = (layers, n_dom, width, slots * blk)
    half = (layers, n_dom // 2, wrows, units)
    small = (layers, n_sub, zrows, units)
    full = (layers, n_dom, n_sub, zrows, units)
    anywhere = pl.BlockSpec(memory_space=pl.ANY)
    upd, fg, weights = pl.pallas_call(
        functools.partial(kernel, n_dom, n_sub),
        out_shape=(
            jax.ShapeDtypeStruct((here, width), BF16),
            jax.ShapeDtypeStruct((here, width), F32),
            jax.ShapeDtypeStruct(full, BF16),
        ),
        in_specs=[smem] * 5 + [vmem] + [anywhere] * 6,
        out_specs=(vmem,) * 3,
        scratch_shapes=[
            pltpu.VMEM(local_matrix.shape, BF16),
            pltpu.VMEM(remote_matrix.shape, BF16),
            pltpu.VMEM(self_weight.shape, BF16),
            pltpu.VMEM(neighbor_weight.shape, BF16),
            pltpu.VMEM(output_weight.shape, BF16),
            pltpu.VMEM(output_cotangent.shape, BF16),
            dma((6,)),
            pltpu.VMEM((here, n_sub * here), BF16),
            pltpu.VMEM((here, n_dom * slots * blk), BF16),
            pltpu.VMEM((layers, here, width), BF16),
            pltpu.VMEM((layers, n_sub, here, width), BF16),
            pltpu.VMEM((layers, here, width), BF16),
            pltpu.VMEM((layers, here, units), F32),
            pltpu.VMEM((layers, here, units), BF16),
            pltpu.VMEM((here, units), F32),
            pltpu.VMEM((n_sub, width, here), F32),
            pltpu.VMEM(edge, BF16),
            pltpu.VMEM(edge, BF16),
            pltpu.VMEM(back, BF16),
            pltpu.VMEM(back, BF16),
            pltpu.VMEM((layers, n_sub + 1, width, here), BF16),
            pltpu.VMEM((layers, 2, n_dom // 2, wrows, units), F32),
            pltpu.VMEM(half, F32),
            pltpu.VMEM(half, BF16),
            pltpu.VMEM(half, BF16),
            pltpu.VMEM(small, BF16),
            pltpu.VMEM(small, BF16),
            dma((layers, n_sub, chunks, 2)),
            dma((layers, n_sub, chunks)),
            dma((layers, n_dom)),
            dma((layers, n_dom)),
            dma((layers, n_dom)),
            dma((layers, n_dom)),
            dma((layers, n_sub, chunks)),
            dma((layers, n_sub + 1, chunks)),
            dma((layers,)),
            dma((layers,)),
            dma((layers, n_dom // 2)),
            dma((layers, n_dom // 2)),
            dma((layers, n_sub)),
            dma((layers, n_sub)),
            dma((layers, n_sub)),
            dma((layers, n_sub)),
            dma((layers, n_dom // 2, n_sub)),
            dma((layers, n_dom // 2, n_sub)),
            dma((layers, n_dom // 2, n_sub)),
            dma((layers, n_dom, n_sub)),
        ],
        compiler_params=pltpu.CompilerParams(
            collective_id=0, has_side_effects=True, vmem_limit_bytes=60 * 1024 * 1024
        ),
    )(local_blocks, remote_blocks, send_blocks, send_counts, partner, features, local_matrix,
      remote_matrix, self_weight, neighbor_weight, output_weight, output_cotangent)
    piece = here // layers

    def rows(shape):
        return pl.BlockSpec((1,) + shape[1:], lambda i: (i,) + (0,) * (len(shape) - 1))

    wide, long = (layers, width, units), (layers, units, width)
    return pl.pallas_call(
        functools.partial(finish, scale, wrows),
        grid=(layers,),
        out_shape=(
            jax.ShapeDtypeStruct((here, width), BF16),
            jax.ShapeDtypeStruct((here, width), F32),
            jax.ShapeDtypeStruct(wide, F32),
            jax.ShapeDtypeStruct(wide, F32),
            jax.ShapeDtypeStruct(long, F32),
        ),
        in_specs=[pl.BlockSpec((piece, width), lambda i: (i, 0))] * 2 + [rows(full)],
        out_specs=(pl.BlockSpec((piece, width), lambda i: (i, 0)),) * 2 + (rows(wide), rows(wide), rows(long)),
        compiler_params=pltpu.CompilerParams(vmem_limit_bytes=60 * 1024 * 1024),
    )(upd, fg, weights)


def solution(mesh):
    whole = ("region", "dom", "sub")
    in_specs = (
        P(whole, None), P(whole, None), P(whole, None, None, None), P(whole, None),
        P(whole, None, None, None), P(whole, None, None), P(whole, None), P("region", None),
        P(), P(), P(), P(whole, None),
    )
    out_specs = (
        P(whole, None), P(whole, None), P("region", None, None), P("region", None, None),
        P("region", None, None),
    )
    return jax.shard_map(local, mesh=mesh, in_specs=in_specs, out_specs=out_specs, check_vma=False)
```
